256 devices in a mesh: row: 8 (over x_hi, y), col: 32 (over x_lo, z, core).
Axes of the slice: x: 4 (x_hi: 2, x_lo: 2; x = x_hi * 2 + x_lo), y: 4, z: 8, core: 2. Of those that a mesh axis runs over, the one named last changes fastest.
Arguments:
- out_grads: bfloat16 [32768, 28672], P('col', 'row'), may hold values from -160 to 160
- old_factor: float32 [28672, 1792], P(('row', 'col')), may hold values from -3 to 3
- inv_factor: float32 [1792, 1792], P('col', 'row'), may hold values from -0.125 to 0.125
- probe_seeds: int32 [64], replicated, may hold values from 0 to 65520
Outputs:
- new_factor: float32 [28672, 1792], P(('row', 'col'))
- chol_panel: float32 [28672, 1792], P(('row', 'col'))
- head_solve: float32 [64, 1792], P(None, 'col')
- probe_rest: float32 [64, 28672], P(None, ('row', 'col'))
The draws below stay inside these ranges and needn't reach their ends.
All inputs are finite; a program needn't handle non-finite values.
Results may differ from the reference program's by a relative error of at most 0.0003.
Values may be sent and summed in bfloat16 or wider, within the bound.
No kernel may reach another device: no remote copies, remote signals or barrier semaphores. Data moves between devices by JAX's collectives and lax.ppermute only.
A program may use at most 192 MiB of HBM per device.

```python
import jax
import jax.numpy as jnp
from jax import lax

FF = 28672
B = 1792
PROBES = 64
TOK_DEV = 1024
TOKENS = 32768
N_COL = 32


def plant(values, own_key, least, high):
    longest = values.shape.index(max(values.shape))
    spots = []
    for shift in (0, 1):
        where = [jax.random.randint(jax.random.fold_in(own_key, axis), (), 0, length) for axis, length in enumerate(values.shape)]
        where[longest] = (where[longest] + shift) % values.shape[longest]
        spots.append(tuple(where))
    return values.at[spots[0]].set(least).at[spots[1]].set(high)


def strengthened(entries, own_key, source, target, parts, factor):
    owner, partner = [(jnp.arange(entries.shape[position]) // (entries.shape[position] // parts)).reshape([-1 if axis == position else 1 for axis in range(entries.ndim)]) for position in (source, target)]
    chosen = jax.random.permutation(own_key, parts)[partner]
    strong = (owner == chosen) | (owner == (partner + parts // 2) % parts)
    return jnp.where(strong, factor * entries, entries)


def shard_levels(own_key, extent, shards, least, top_value):
    def one(position, shards_of):
        steps = jax.random.uniform(jax.random.fold_in(jax.random.fold_in(own_key, 6), position), (shards_of,), jnp.float32, least / len(shards), top_value / len(shards))
        return jnp.repeat(jnp.exp(steps), extent[position] // shards_of).reshape((-1,) + (1,) * (len(extent) - position - 1))

    gain = one(*shards[0])
    for cut in shards[1:]:
        gain = gain * one(*cut)
    return gain


def scatter_about(rng, dims, scale, reach, pieces=(), kind=jnp.bfloat16):
    array = scale * jax.random.normal(rng, dims, jnp.float32)
    if pieces:
        array = array * shard_levels(rng, dims, pieces, -0.22, 0.18)
    return jnp.clip(array, -reach, reach).astype(kind)


def bell_draw_with(stream_key, dims, width, bound, split, heavy, held_as=jnp.bfloat16):
    drawn = width * jax.random.normal(stream_key, dims, jnp.float32)
    if split:
        drawn = drawn * shard_levels(stream_key, dims, split, -0.22, 0.18)
    return jnp.clip(strengthened(drawn, jax.random.fold_in(stream_key, 3), *heavy), -bound, bound).astype(held_as)


def setup_inputs(seed: int = 0) -> dict:
    keys = jax.random.split(jax.random.key(seed), 5)
    return {
        "out_grads": bell_draw_with(keys[0], (TOKENS, FF), (TOKENS ** 0.25), 160.0, ((0, 32), (1, 8)), (0, 1, 32, 2.75)),
        "old_factor": scatter_about(keys[1], (FF, B), 0.2, 3.0, ((0, 256),), jnp.float32),
        "inv_factor": scatter_about(keys[2], (B, B), B ** -0.5, 0.125, ((0, 32), (1, 8)), jnp.float32),
        "probe_seeds": plant(jax.random.randint(keys[3], (PROBES,), 0, 65521), jax.random.fold_in(keys[3], 1), 0, 65520).astype(jnp.int32),
    }


def rademacher(seeds, index):
    mixed = (seeds[:, None] * 179 + index[None, :] * 7 + 12345) % 65521
    folded = (mixed * (mixed % 32749)) % 65519
    parity = (folded // 13) % 2
    return 1.0 - 2.0 * parity.astype(jnp.float32)


def reference(out_grads, old_factor, inv_factor, probe_seeds):
    probes = rademacher(probe_seeds, jnp.arange(FF, dtype=jnp.int32))
    blocks = out_grads.reshape(N_COL, TOK_DEV, FF)

    def accumulate(total, block):
        wide = block.astype(jnp.float32)
        part = jnp.dot(wide.T, wide[:, :B], precision=lax.Precision.HIGHEST)
        return total + part, None

    summed, _ = lax.scan(accumulate, jnp.zeros((FF, B), jnp.float32), blocks)
    new_factor = 0.9 * old_factor + (0.1 / TOKENS) * summed
    on_diag = jnp.arange(FF, dtype=jnp.int32)[:, None] == jnp.arange(B, dtype=jnp.int32)[None, :]
    damped = new_factor + jnp.where(on_diag, 1.0, 0.0).astype(jnp.float32)
    chol_panel = jnp.dot(damped, inv_factor, precision=lax.Precision.HIGHEST)
    head_solve = jnp.dot(probes[:, :B], inv_factor, precision=lax.Precision.HIGHEST)
    probe_rest = probes - jnp.dot(head_solve, chol_panel.T, precision=lax.Precision.HIGHEST)
    return new_factor, chol_panel, head_solve, probe_rest
```

```python
import functools

import jax
import jax.numpy as jnp
from jax import lax
from jax.experimental import pallas as pl
from jax.experimental.pallas import tpu as pltpu
from jax.sharding import Mesh
from jax.sharding import PartitionSpec as P

F32 = jnp.float32
HIGH = lax.Precision.HIGH
ROW = ("xh", "y")
SWAP = [(0, 1), (1, 0)]
SPLIT = 512
TILE = 256


def rademacher(seeds, index):
    mixed = (seeds[:, None] * 179 + index[None, :] * 7 + 12345) % 65521
    folded = mixed * (mixed % 32749) % 65519
    parity = folded // 13 % 2
    return 1.0 - 2.0 * parity.astype(F32)


def gather_rounds(own):
    xh, y = lax.axis_index("xh"), lax.axis_index("y")
    up = [(i, (i + 1) % 4) for i in range(4)]
    down = [(i, (i + 3) % 4) for i in range(4)]
    across = lax.ppermute(own, "xh", SWAP)
    above = lax.ppermute(own, "y", up)
    below = lax.ppermute(own, "y", down)
    across_above = lax.ppermute(above, "xh", SWAP)
    across_below = lax.ppermute(across, "y", down)
    twice = lax.ppermute(above, "y", up)
    cut = own.shape[0] // 2
    across_twice = jnp.concatenate(
        [
            lax.ppermute(across_above[:cut], "y", up),
            lax.ppermute(across_below[cut:], "y", down),
        ],
        axis=0,
    )
    here, there = xh * 4, (1 - xh) * 4
    last, following, opposite = (y + 3) % 4, (y + 1) % 4, (y + 2) % 4
    return [
        (here + y, own),
        (there + y, across),
        (here + last, above),
        (here + following, below),
        (here + opposite, twice),
        (there + last, across_above),
        (there + following, across_below),
        (there + opposite, across_twice),
    ]


def scatter(mine, partner):
    ways = lax.axis_size("xh") * lax.axis_size("y")
    share = 2 * mine.shape[0] // ways
    me = lax.axis_index(ROW)
    first = partner[:share]
    own = jnp.where(me == 0, first, jnp.zeros_like(first))
    for r in list(range(ways // 2, ways)) + list(range(1, ways // 2)):
        source = partner if r < ways // 2 else mine
        start = r % (ways // 2) * share
        own = own + lax.ppermute(source[start : start + share], ROW, [(0, r)])
    return own


def gram_body(count, where_ref, own_ref, other_ref, *refs):
    pieces, out_ref, head_ref = refs[:count], refs[-2], refs[-1]
    tokens = own_ref.shape[0]
    share = pieces[0].shape[0]

    @pl.when(pl.program_id(0) == 0)
    def _():
        for n, piece in enumerate(pieces):
            start = pl.multiple_of(where_ref[n + 1] * share, share)
            head_ref[pl.ds(start, share), :] = piece[...]

    contract = (((0,), (0,)), ((), ()))
    first = lax.dot_general(
        own_ref[...], head_ref[:tokens], contract, preferred_element_type=F32
    )
    second = lax.dot_general(
        other_ref[...], head_ref[tokens:], contract, preferred_element_type=F32
    )
    out_ref[...] = (first + second).reshape(out_ref.shape)


def gram(own, other, head, after, start, tile, out_shape, out_block, out_index):
    tokens = own.shape[0]
    places = jnp.stack([start] + [(place + 4) % 8 for place, _ in head]).astype(jnp.int32)
    pieces = [piece for _, piece in head]
    share, width = pieces[0].shape
    block = pl.BlockSpec((tokens, tile), lambda i, s: (0, s[0] + i))
    whole = pl.BlockSpec((share, width), lambda i, s: (0, 0))
    size = 1
    for extent in out_shape:
        size *= extent
    rows = size // width
    return pl.pallas_call(
        functools.partial(gram_body, len(pieces)),
        grid_spec=pltpu.PrefetchScalarGridSpec(
            num_scalar_prefetch=1,
            grid=(rows // tile,),
            in_specs=[block, block]
            + [whole] * len(pieces)
            + [pl.BlockSpec(memory_space=pl.ANY)] * len(after),
            out_specs=pl.BlockSpec(out_block, out_index),
            scratch_shapes=[pltpu.VMEM((share * len(pieces), width), jnp.bfloat16)],
        ),
        out_shape=jax.ShapeDtypeStruct(out_shape, F32),
        compiler_params=pltpu.CompilerParams(vmem_limit_bytes=48 * 1024 * 1024),
        cost_estimate=pl.CostEstimate(
            flops=4 * tokens * rows * width,
            bytes_accessed=4 * tokens * rows + 4 * tokens * width + 4 * rows * width,
            transcendentals=0,
        ),
    )(places, own, other, *pieces, *after)


def gather_y(own):
    y = lax.axis_index("y")
    up = [(i, (i + 1) % 4) for i in range(4)]
    down = [(i, (i + 3) % 4) for i in range(4)]
    above = lax.ppermute(own, "y", up)
    below = lax.ppermute(own, "y", down)
    first = lax.ppermute(above[0], "y", up)
    second = lax.ppermute(below[1], "y", down)
    twice = jnp.stack([first, second])
    return [(y, own), ((y + 3) % 4, above), ((y + 1) % 4, below), ((y + 2) % 4, twice)]


def local(out_grads, old_factor, inv_factor, probe_seeds):
    core = lax.axis_index("c")
    side = lax.axis_index("xl")
    ranks = lax.axis_size("z")
    own_rows, block_w = old_factor.shape
    half = block_w // 2
    chip_rows = 2 * own_rows
    tokens_all = out_grads.shape[0] * 2 * ranks * 2

    keep = lax.dynamic_slice_in_dim(out_grads, core * half, half, 1)
    give = lax.dynamic_slice_in_dim(out_grads, (1 - core) * half, half, 1)
    got = lax.ppermute(give, ("xh", "y", "c"), SWAP)
    own_b = scatter(keep[:, :SPLIT], got[:, :SPLIT])
    own_a = scatter(keep[:, SPLIT:], got[:, SPLIT:])
    other_grads = lax.ppermute(out_grads, "c", SWAP)
    head_b = gather_rounds(own_b)
    head_a = gather_rounds(own_a)
    held = lax.all_gather(inv_factor, ("xh", "xl", "z", "c"), axis=0, tiled=True)
    held = lax.dynamic_slice_in_dim(held.reshape(2, block_w, -1), core * half, half, 1)

    group = ranks * chip_rows
    width_b, width_a = SPLIT, half - SPLIT
    part_b = gram(
        out_grads, other_grads, head_b, [own_a], 0 * core, 4 * chip_rows,
        (ranks, 2, chip_rows, width_b), (4, 1, chip_rows, width_b),
        lambda i, s: (i % 2, i // 2, 0, 0),
    )
    sum_b = lax.psum_scatter(
        part_b.reshape(2 * group, width_b), "z", scatter_dimension=0, tiled=True
    )

    def rows_of(which, after):
        tiles = group // TILE
        return gram(
            out_grads, other_grads, head_a, after, which * tiles, TILE,
            (group, width_a), (TILE, width_a), lambda i, s: (i, 0),
        )

    give_a = rows_of(1 - side, [])
    held, _ = lax.optimization_barrier((held, head_a[-1][1]))
    rest = gather_y(held)
    keep_a = rows_of(side, [])
    got_a = lax.ppermute(give_a, "xl", SWAP)
    got_a, rest_pieces = lax.optimization_barrier((got_a, [piece for _, piece in rest]))
    sum_a = lax.psum_scatter(keep_a + got_a, "z", scatter_dimension=0, tiled=True)
    far_b = lax.dynamic_slice_in_dim(sum_b, (1 - side) * chip_rows, chip_rows, 0)
    near_b = lax.dynamic_slice_in_dim(sum_b, side * chip_rows, chip_rows, 0)
    sum_b = near_b + lax.ppermute(far_b, "xl", SWAP)

    inverse = jnp.zeros((4,) + held.shape, F32)
    for (place, _), piece in zip(rest, rest_pieces):
        inverse = lax.dynamic_update_index_in_dim(inverse, piece, place, 0)
    inverse = jnp.transpose(inverse, (2, 1, 0, 3)).reshape(half, block_w)

    old_keep = lax.dynamic_slice_in_dim(old_factor, core * half, half, 1)
    old_give = lax.dynamic_slice_in_dim(old_factor, (1 - core) * half, half, 1)
    old_got = lax.ppermute(old_give, "c", SWAP)
    old_half = jnp.where(
        core == 0,
        jnp.concatenate([old_keep, old_got], axis=0),
        jnp.concatenate([old_got, old_keep], axis=0),
    )
    chip = lax.axis_index(("xh", "y", "xl", "z"))
    columns = core * half + jnp.arange(half, dtype=jnp.int32)
    probe_head = rademacher(probe_seeds, columns)
    head_part = jnp.dot(probe_head, inverse, precision=HIGH)
    head_full = head_part + lax.ppermute(head_part, "c", SWAP)

    row_index = chip * chip_rows + jnp.arange(chip_rows, dtype=jnp.int32)
    on_diag = jnp.where(row_index[:, None] == columns[None, :], 1.0, 0.0).astype(F32)
    factor_b = 0.9 * old_half[:, :SPLIT] + 0.1 / tokens_all * sum_b
    panel_b = jnp.dot(factor_b + on_diag[:, :SPLIT], inverse[:SPLIT], precision=HIGH)
    sum_a, panel_b = lax.optimization_barrier((sum_a, panel_b))
    factor_a = 0.9 * old_half[:, SPLIT:] + 0.1 / tokens_all * sum_a
    panel_a = jnp.dot(factor_a + on_diag[:, SPLIT:], inverse[SPLIT:], precision=HIGH)
    panel_part = panel_b + panel_a
    factor_half = jnp.concatenate([factor_b, factor_a], axis=1)
    theirs, ours = (1 - core) * own_rows, core * own_rows
    factor_keep = lax.dynamic_slice_in_dim(factor_half, ours, own_rows, 0)
    factor_got = lax.ppermute(
        lax.dynamic_slice_in_dim(factor_half, theirs, own_rows, 0), "c", SWAP
    )
    new_factor = jnp.where(
        core == 0,
        jnp.concatenate([factor_keep, factor_got], axis=1),
        jnp.concatenate([factor_got, factor_keep], axis=1),
    )
    panel_got = lax.ppermute(
        lax.dynamic_slice_in_dim(panel_part, theirs, own_rows, 0), "c", SWAP
    )
    chol_panel = lax.dynamic_slice_in_dim(panel_part, ours, own_rows, 0) + panel_got

    own_index = lax.dynamic_slice_in_dim(row_index, ours, own_rows, 0)
    probe_rest = rademacher(probe_seeds, own_index) - lax.dot_general(
        head_full, chol_panel, (((1,), (1,)), ((), ())), precision=HIGH
    )
    share = block_w // (2 * ranks * 2)
    place = lax.axis_index(("xl", "z", "c")) * share
    head_solve = lax.dynamic_slice_in_dim(head_full, place, share, 1)
    return new_factor, chol_panel, head_solve, probe_rest


def solution(mesh):
    fine = Mesh(mesh.devices.reshape(2, 4, 2, 8, 2), ("xh", "y", "xl", "z", "c"))
    col = ("xl", "z", "c")
    every = ROW + col
    return jax.shard_map(
        local,
        mesh=fine,
        in_specs=(P(col, ROW), P(every, None), P(col, ROW), P()),
        out_specs=(P(every, None), P(every, None), P(None, col), P(None, every)),
        check_vma=False,
    )
```

```python
import functools

import jax
import jax.numpy as jnp
from jax import lax
from jax.experimental import pallas as pl
from jax.experimental.pallas import tpu as pltpu
from jax.sharding import Mesh
from jax.sharding import PartitionSpec as P

F32 = jnp.float32
HIGH = lax.Precision.HIGH
ROW = ("xh", "y")
SWAP = [(0, 1), (1, 0)]
SPLIT = 512
TILE = 256


def rademacher(seeds, index):
    mixed = (seeds[:, None] * 179 + index[None, :] * 7 + 12345) % 65521
    folded = mixed * (mixed % 32749) % 65519
    parity = folded // 13 % 2
    return 1.0 - 2.0 * parity.astype(F32)


def once(value, after):
    mark = after[0, 0]
    return jnp.where(mark == mark, value, jnp.zeros_like(value))


def gather_rounds(own):
    xh, y = lax.axis_index("xh"), lax.axis_index("y")
    up = [(i, (i + 1) % 4) for i in range(4)]
    down = [(i, (i + 3) % 4) for i in range(4)]
    across = lax.ppermute(own, "xh", SWAP)
    above = lax.ppermute(own, "y", up)
    below = lax.ppermute(own, "y", down)
    across_above = lax.ppermute(above, "xh", SWAP)
    across_below = lax.ppermute(across, "y", down)
    twice = lax.ppermute(above, "y", up)
    cut = own.shape[0] // 2
    across_twice = jnp.concatenate(
        [
            lax.ppermute(across_above[:cut], "y", up),
            lax.ppermute(across_below[cut:], "y", down),
        ],
        axis=0,
    )
    here, there = xh * 4, (1 - xh) * 4
    last, following, opposite = (y + 3) % 4, (y + 1) % 4, (y + 2) % 4
    return [
        (here + y, own),
        (there + y, across),
        (here + last, above),
        (here + following, below),
        (here + opposite, twice),
        (there + last, across_above),
        (there + following, across_below),
        (there + opposite, across_twice),
    ]


def scatter(mine, partner):
    xh, y, me = lax.axis_index("xh"), lax.axis_index("y"), lax.axis_index(ROW)
    share = mine.shape[0] // 4
    own_cols, partner_cols = mine[:, :SPLIT], partner[:, :SPLIT]
    two = 2 * share
    near = jnp.where(me == 0, partner_cols[two : two + share], jnp.zeros_like(own_cols[:share]))
    pair = jnp.concatenate(
        [near + lax.ppermute(partner_cols[:share], ROW, [(0, 2)]),
         jnp.where(me == 0, partner_cols[two + share :], jnp.zeros_like(near))], axis=0
    )
    pair = pair + lax.ppermute(own_cols[:two], ROW, [(0, 1)])
    pair = pair + lax.ppermute(own_cols[two:], ROW, [(0, 3)])
    direct = lax.ppermute(partner_cols[share:two], ROW, [(0, 6)])
    last = mine[:, SPLIT:]
    far = lax.ppermute(last, ROW, [(0, 4)])
    crossed = lax.ppermute(pair[share:], "xh", [(0, 1)])
    own_b = jnp.where(xh == 0, pair[:share], crossed + direct)
    source = jnp.where(xh == 0, partner[:, SPLIT:], far)
    own_a = jnp.where(y == 0, source[:share], jnp.zeros_like(source[:share]))
    for r in (1, 3, 2):
        own_a = own_a + lax.ppermute(source[r * share : (r + 1) * share], "y", [(0, r)])
    return own_b, own_a


def place_b(owner):
    xh, y = owner // 4, owner % 4
    return jnp.where(y % 2 == 1, y - 1, 6 - y) + xh


def place_a(owner):
    return (owner + 4) % 8


def gram_body(count, where_ref, own_ref, other_ref, *refs):
    pieces, out_ref, head_ref = refs[:count], refs[-2], refs[-1]
    tokens = own_ref.shape[0]
    share = pieces[0].shape[0]

    @pl.when(pl.program_id(0) == 0)
    def _():
        for n, piece in enumerate(pieces):
            start = pl.multiple_of(where_ref[n + 1] * share, share)
            head_ref[pl.ds(start, share), :] = piece[...]

    contract = (((0,), (0,)), ((), ()))
    first = lax.dot_general(
        own_ref[...], head_ref[:tokens], contract, preferred_element_type=F32
    )
    second = lax.dot_general(
        other_ref[...], head_ref[tokens:], contract, preferred_element_type=F32
    )
    out_ref[...] = (first + second).reshape(out_ref.shape)


def gram(own, other, head, place, start, tile, out_shape, out_block, out_index):
    tokens = own.shape[0]
    places = jnp.stack([start] + [place(owner) for owner, _ in head]).astype(jnp.int32)
    pieces = [piece for _, piece in head]
    share, width = pieces[0].shape
    block = pl.BlockSpec((tokens, tile), lambda i, s: (0, s[0] + i))
    whole = pl.BlockSpec((share, width), lambda i, s: (0, 0))
    size = 1
    for extent in out_shape:
        size *= extent
    rows = size // width
    return pl.pallas_call(
        functools.partial(gram_body, len(pieces)),
        grid_spec=pltpu.PrefetchScalarGridSpec(
            num_scalar_prefetch=1,
            grid=(rows // tile,),
            in_specs=[block, block] + [whole] * len(pieces),
            out_specs=pl.BlockSpec(out_block, out_index),
            scratch_shapes=[pltpu.VMEM((share * len(pieces), width), jnp.bfloat16)],
        ),
        out_shape=jax.ShapeDtypeStruct(out_shape, F32),
        compiler_params=pltpu.CompilerParams(vmem_limit_bytes=48 * 1024 * 1024),
        cost_estimate=pl.CostEstimate(
            flops=4 * tokens * rows * width,
            bytes_accessed=4 * tokens * rows + 4 * tokens * width + 4 * rows * width,
            transcendentals=0,
        ),
    )(places, own, other, *pieces)


def shifted(value, step):
    return lax.ppermute(value, "y", [(i, (i + step) % 4) for i in range(4)])


def local(out_grads, old_factor, inv_factor, probe_seeds):
    core = lax.axis_index("c")
    side = lax.axis_index("xl")
    ranks = lax.axis_size("z")
    own_rows, block_w = old_factor.shape
    half = block_w // 2
    chip_rows = 2 * own_rows
    tokens_all = out_grads.shape[0] * 2 * ranks * 2

    keep = lax.dynamic_slice_in_dim(out_grads, core * half, half, 1)
    give = lax.dynamic_slice_in_dim(out_grads, (1 - core) * half, half, 1)
    got = lax.ppermute(give, ("xh", "y", "c"), SWAP)
    other_grads = lax.ppermute(out_grads, "c", SWAP)
    own_b, own_a = scatter(keep, got)
    head_b = gather_rounds(once(own_b, own_a))
    head_a = gather_rounds(once(own_a, head_b[5][1]))
    held = lax.all_gather(inv_factor, ("xh", "xl", "z", "c"), axis=0, tiled=True)

    group = ranks * chip_rows
    width_b, width_a = SPLIT, half - SPLIT
    part_b = gram(
        out_grads, other_grads, head_b, place_b, 0 * core, 4 * chip_rows,
        (ranks, 2, chip_rows, width_b), (4, 1, chip_rows, width_b),
        lambda i, s: (i % 2, i // 2, 0, 0),
    )
    sum_b = lax.psum_scatter(
        part_b.reshape(2 * group, width_b), "z", scatter_dimension=0, tiled=True
    )

    def rows_of(which):
        tiles = group // TILE
        return gram(
            out_grads, other_grads, head_a, place_a, which * tiles, TILE,
            (group, width_a), (TILE, width_a), lambda i, s: (i, 0),
        )

    give_a = rows_of(1 - side)
    keep_a = rows_of(side)
    got_a = lax.ppermute(give_a, "xl", SWAP)

    held = once(held, keep_a).reshape(2, block_w, -1)
    held = lax.dynamic_slice_in_dim(held, core * half, half, 1)
    above, below = shifted(held, 1), shifted(held, 3)
    part_a = keep_a + once(once(got_a, above[0]), below[0])
    twice = jnp.stack([
        shifted(once(above[0], part_a), 1), shifted(once(below[1], part_a), 3)
    ])
    y = lax.axis_index("y")
    rest = [(y, held), ((y + 3) % 4, above), ((y + 1) % 4, below), ((y + 2) % 4, twice)]
    sum_a = lax.psum_scatter(part_a, "z", scatter_dimension=0, tiled=True)
    far_b = lax.dynamic_slice_in_dim(sum_b, (1 - side) * chip_rows, chip_rows, 0)
    near_b = lax.dynamic_slice_in_dim(sum_b, side * chip_rows, chip_rows, 0)
    sum_b = near_b + lax.ppermute(far_b, "xl", SWAP)

    inverse = jnp.zeros((4,) + rest[0][1].shape, F32)
    for place, piece in rest:
        inverse = lax.dynamic_update_index_in_dim(inverse, piece, place, 0)
    inverse = jnp.transpose(inverse, (2, 1, 0, 3)).reshape(half, block_w)

    old_keep = lax.dynamic_slice_in_dim(old_factor, core * half, half, 1)
    old_give = lax.dynamic_slice_in_dim(old_factor, (1 - core) * half, half, 1)
    old_got = lax.ppermute(old_give, "c", SWAP)
    old_half = jnp.where(
        core == 0,
        jnp.concatenate([old_keep, old_got], axis=0),
        jnp.concatenate([old_got, old_keep], axis=0),
    )
    chip = lax.axis_index(("xh", "y", "xl", "z"))
    columns = core * half + jnp.arange(half, dtype=jnp.int32)
    probe_head = rademacher(probe_seeds, columns)
    head_part = jnp.dot(probe_head, inverse, precision=HIGH)
    head_full = head_part + lax.ppermute(head_part, "c", SWAP)

    row_index = chip * chip_rows + jnp.arange(chip_rows, dtype=jnp.int32)
    on_diag = jnp.where(row_index[:, None] == columns[None, :], 1.0, 0.0).astype(F32)
    factor_b = 0.9 * old_half[:, :SPLIT] + 0.1 / tokens_all * sum_b
    panel_b = jnp.dot(factor_b + on_diag[:, :SPLIT], inverse[:SPLIT], precision=HIGH)
    sum_a, panel_b = lax.optimization_barrier((sum_a, panel_b))
    factor_a = 0.9 * old_half[:, SPLIT:] + 0.1 / tokens_all * sum_a
    panel_a = jnp.dot(factor_a + on_diag[:, SPLIT:], inverse[SPLIT:], precision=HIGH)
    panel_part = panel_b + panel_a
    factor_half = jnp.concatenate([factor_b, factor_a], axis=1)
    theirs, ours = (1 - core) * own_rows, core * own_rows
    factor_keep = lax.dynamic_slice_in_dim(factor_half, ours, own_rows, 0)
    factor_got = lax.ppermute(
        lax.dynamic_slice_in_dim(factor_half, theirs, own_rows, 0), "c", SWAP
    )
    new_factor = jnp.where(
        core == 0,
        jnp.concatenate([factor_keep, factor_got], axis=1),
        jnp.concatenate([factor_got, factor_keep], axis=1),
    )
    panel_got = lax.ppermute(
        lax.dynamic_slice_in_dim(panel_part, theirs, own_rows, 0), "c", SWAP
    )
    chol_panel = lax.dynamic_slice_in_dim(panel_part, ours, own_rows, 0) + panel_got

    own_index = lax.dynamic_slice_in_dim(row_index, ours, own_rows, 0)
    probe_rest = rademacher(probe_seeds, own_index) - lax.dot_general(
        head_full, chol_panel, (((1,), (1,)), ((), ())), precision=HIGH
    )
    share = block_w // (2 * ranks * 2)
    place = lax.axis_index(("xl", "z", "c")) * share
    head_solve = lax.dynamic_slice_in_dim(head_full, place, share, 1)
    return new_factor, chol_panel, head_solve, probe_rest


def solution(mesh):
    fine = Mesh(mesh.devices.reshape(2, 4, 2, 8, 2), ("xh", "y", "xl", "z", "c"))
    col = ("xl", "z", "c")
    every = ROW + col
    return jax.shard_map(
        local,
        mesh=fine,
        in_specs=(P(col, ROW), P(every, None), P(col, ROW), P()),
        out_specs=(P(every, None), P(every, None), P(None, col), P(None, every)),
        check_vma=False,
    )
```

```python
import functools

import jax
import jax.numpy as jnp
from jax import lax
from jax.experimental import pallas as pl
from jax.experimental.pallas import tpu as pltpu
from jax.sharding import Mesh
from jax.sharding import PartitionSpec as P

F32 = jnp.float32
HIGH = lax.Precision.HIGH
ROW = ("xh", "y")
SWAP = [(0, 1), (1, 0)]
SPLIT = 512
TILE = 256


def rademacher(seeds, index):
    mixed = (seeds[:, None] * 179 + index[None, :] * 7 + 12345) % 65521
    folded = mixed * (mixed % 32749) % 65519
    parity = folded // 13 % 2
    return 1.0 - 2.0 * parity.astype(F32)


def once(value, after):
    mark = after[0, 0]
    return jnp.where(mark == mark, value, jnp.zeros_like(value))


def gather_rounds(own, after):
    xh, y = lax.axis_index("xh"), lax.axis_index("y")
    up = [(i, (i + 1) % 4) for i in range(4)]
    down = [(i, (i + 3) % 4) for i in range(4)]
    across = lax.ppermute(own, "xh", SWAP)
    above = lax.ppermute(own, "y", up)
    below = lax.ppermute(own, "y", down)
    first_round = [across, above, below]
    above = once(above, after)
    across_above = lax.ppermute(above, "xh", SWAP)
    across_below = lax.ppermute(across, "y", down)
    twice = lax.ppermute(above, "y", up)
    cut = own.shape[0] // 2
    across_twice = jnp.concatenate(
        [
            lax.ppermute(across_above[:cut], "y", up),
            lax.ppermute(across_below[cut:], "y", down),
        ],
        axis=0,
    )
    here, there = xh * 4, (1 - xh) * 4
    last, following, opposite = (y + 3) % 4, (y + 1) % 4, (y + 2) % 4
    return [
        (here + y, own),
        (there + y, across),
        (here + last, above),
        (here + following, below),
        (here + opposite, twice),
        (there + last, across_above),
        (there + following, across_below),
        (there + opposite, across_twice),
    ], first_round


def scatter(mine, partner):
    xh, y, me = lax.axis_index("xh"), lax.axis_index("y"), lax.axis_index(ROW)
    share = mine.shape[0] // 4
    own_cols, partner_cols = mine[:, :SPLIT], partner[:, :SPLIT]
    two = 2 * share
    near = jnp.where(me == 0, partner_cols[two : two + share], jnp.zeros_like(own_cols[:share]))
    pair = jnp.concatenate(
        [near + lax.ppermute(own_cols[two + share :], ROW, [(0, 2)]),
         jnp.where(me == 0, partner_cols[two + share :], jnp.zeros_like(near))], axis=0
    )
    pair = pair + lax.ppermute(own_cols[:two], ROW, [(0, 1)])
    pair = pair + lax.ppermute(partner_cols[:two], ROW, [(0, 3)])
    direct = lax.ppermute(own_cols[two : two + share], ROW, [(0, 6)])
    last = mine[:, SPLIT:]
    far = lax.ppermute(last, ROW, [(0, 4)])
    crossed = lax.ppermute(pair[share:], "xh", [(0, 1)])
    own_b = jnp.where(xh == 0, pair[:share], crossed + direct)
    source = once(jnp.where(xh == 0, partner[:, SPLIT:], far), pair)
    own_a = jnp.where(y == 0, source[:share], jnp.zeros_like(source[:share]))
    for r in (1, 3, 2):
        own_a = own_a + lax.ppermute(source[r * share : (r + 1) * share], "y", [(0, r)])
    return once(own_b, far), own_a


def place_b(owner):
    xh, y = owner // 4, owner % 4
    start = jnp.where(y == 0, 6, jnp.where(y == 1, 0, 4))
    return jnp.where(y == 2, 3 - xh, start + xh)


def place_a(owner):
    return (owner + 4) % 8


def gram_body(count, where_ref, own_ref, other_ref, *refs):
    pieces, out_ref, head_ref = refs[:count], refs[-2], refs[-1]
    tokens = own_ref.shape[0]
    share = pieces[0].shape[0]

    @pl.when(pl.program_id(0) == 0)
    def _():
        for n, piece in enumerate(pieces):
            start = pl.multiple_of(where_ref[n + 1] * share, share)
            head_ref[pl.ds(start, share), :] = piece[...]

    contract = (((0,), (0,)), ((), ()))
    first = lax.dot_general(
        own_ref[...], head_ref[:tokens], contract, preferred_element_type=F32
    )
    second = lax.dot_general(
        other_ref[...], head_ref[tokens:], contract, preferred_element_type=F32
    )
    out_ref[...] = (first + second).reshape(out_ref.shape)


def gram(own, other, head, after, place, start, tile, out_shape, out_block, out_index):
    tokens = own.shape[0]
    places = jnp.stack([start] + [place(owner) for owner, _ in head]).astype(jnp.int32)
    pieces = [piece for _, piece in head]
    share, width = pieces[0].shape
    block = pl.BlockSpec((tokens, tile), lambda i, s: (0, s[0] + i))
    whole = pl.BlockSpec((share, width), lambda i, s: (0, 0))
    size = 1
    for extent in out_shape:
        size *= extent
    rows = size // width
    return pl.pallas_call(
        functools.partial(gram_body, len(pieces)),
        grid_spec=pltpu.PrefetchScalarGridSpec(
            num_scalar_prefetch=1,
            grid=(rows // tile,),
            in_specs=[block, block]
            + [whole] * len(pieces)
            + [pl.BlockSpec(memory_space=pl.ANY)] * len(after),
            out_specs=pl.BlockSpec(out_block, out_index),
            scratch_shapes=[pltpu.VMEM((share * len(pieces), width), jnp.bfloat16)],
        ),
        out_shape=jax.ShapeDtypeStruct(out_shape, F32),
        compiler_params=pltpu.CompilerParams(vmem_limit_bytes=48 * 1024 * 1024),
        cost_estimate=pl.CostEstimate(
            flops=4 * tokens * rows * width,
            bytes_accessed=4 * tokens * rows + 4 * tokens * width + 4 * rows * width,
            transcendentals=0,
        ),
    )(places, own, other, *pieces, *after)


def shifted(value, step):
    return lax.ppermute(value, "y", [(i, (i + step) % 4) for i in range(4)])


def local(out_grads, old_factor, inv_factor, probe_seeds):
    core = lax.axis_index("c")
    side = lax.axis_index("xl")
    ranks = lax.axis_size("z")
    own_rows, block_w = old_factor.shape
    half = block_w // 2
    chip_rows = 2 * own_rows
    tokens_all = out_grads.shape[0] * 2 * ranks * 2

    other_grads = lax.ppermute(out_grads, "c", SWAP)
    keep = lax.dynamic_slice_in_dim(out_grads, core * half, half, 1)
    got = lax.dynamic_slice_in_dim(other_grads, core * half, half, 1)
    own_b, own_a = scatter(keep, got)
    head_b, _ = gather_rounds(own_b, own_a)
    head_a, first_a = gather_rounds(once(own_a, head_b[5][1]), head_b[7][1])
    held = lax.all_gather(inv_factor, ("xh", "xl", "z", "c"), axis=0, tiled=True)

    group = ranks * chip_rows
    width_b, width_a = SPLIT, half - SPLIT
    part_b = gram(
        out_grads, other_grads, head_b, first_a, place_b, 0 * core, 4 * chip_rows,
        (ranks, 2, chip_rows, width_b), (4, 1, chip_rows, width_b),
        lambda i, s: (i % 2, i // 2, 0, 0),
    )
    sum_b = lax.psum_scatter(
        part_b.reshape(2 * group, width_b), "z", scatter_dimension=0, tiled=True
    )

    def rows_of(which):
        tiles = group // TILE
        return gram(
            out_grads, other_grads, head_a, [], place_a, which * tiles, TILE,
            (group, width_a), (TILE, width_a), lambda i, s: (i, 0),
        )

    give_a = rows_of(1 - side)
    keep_a = rows_of(side)
    got_a = lax.ppermute(give_a, "xl", SWAP)

    held = lax.dynamic_slice_in_dim(held.reshape(2, block_w, -1), core * half, half, 1)
    held = once(held, keep_a)
    above, below = shifted(held, 1), shifted(held, 3)
    part_a = keep_a + once(once(got_a, above[0]), below[0])
    twice = jnp.stack([
        shifted(once(above[0], got_a), 1), shifted(once(below[1], got_a), 3)
    ])
    y = lax.axis_index("y")
    rest = [(y, held), ((y + 3) % 4, above), ((y + 1) % 4, below), ((y + 2) % 4, twice)]
    sum_a = lax.psum_scatter(part_a, "z", scatter_dimension=0, tiled=True)
    far_b = lax.dynamic_slice_in_dim(sum_b, (1 - side) * chip_rows, chip_rows, 0)
    near_b = lax.dynamic_slice_in_dim(sum_b, side * chip_rows, chip_rows, 0)
    sum_b = near_b + lax.ppermute(far_b, "xl", SWAP)

    inverse = jnp.zeros((4,) + rest[0][1].shape, F32)
    for place, piece in rest:
        inverse = lax.dynamic_update_index_in_dim(inverse, piece, place, 0)
    inverse = jnp.transpose(inverse, (2, 1, 0, 3)).reshape(half, block_w)

    old_keep = lax.dynamic_slice_in_dim(old_factor, core * half, half, 1)
    old_give = lax.dynamic_slice_in_dim(old_factor, (1 - core) * half, half, 1)
    old_got = lax.ppermute(old_give, "c", SWAP)
    old_half = jnp.where(
        core == 0,
        jnp.concatenate([old_keep, old_got], axis=0),
        jnp.concatenate([old_got, old_keep], axis=0),
    )
    chip = lax.axis_index(("xh", "y", "xl", "z"))
    columns = core * half + jnp.arange(half, dtype=jnp.int32)
    probe_head = rademacher(probe_seeds, columns)
    head_part = jnp.dot(probe_head, inverse, precision=HIGH)
    head_full = head_part + lax.ppermute(head_part, "c", SWAP)

    row_index = chip * chip_rows + jnp.arange(chip_rows, dtype=jnp.int32)
    on_diag = jnp.where(row_index[:, None] == columns[None, :], 1.0, 0.0).astype(F32)
    factor_b = 0.9 * old_half[:, :SPLIT] + 0.1 / tokens_all * sum_b
    panel_b = jnp.dot(factor_b + on_diag[:, :SPLIT], inverse[:SPLIT], precision=HIGH)
    sum_a, panel_b = lax.optimization_barrier((sum_a, panel_b))
    factor_a = 0.9 * old_half[:, SPLIT:] + 0.1 / tokens_all * sum_a
    panel_a = jnp.dot(factor_a + on_diag[:, SPLIT:], inverse[SPLIT:], precision=HIGH)
    panel_part = panel_b + panel_a
    factor_half = jnp.concatenate([factor_b, factor_a], axis=1)
    theirs, ours = (1 - core) * own_rows, core * own_rows
    factor_keep = lax.dynamic_slice_in_dim(factor_half, ours, own_rows, 0)
    factor_got = lax.ppermute(
        lax.dynamic_slice_in_dim(factor_half, theirs, own_rows, 0), "c", SWAP
    )
    new_factor = jnp.where(
        core == 0,
        jnp.concatenate([factor_keep, factor_got], axis=1),
        jnp.concatenate([factor_got, factor_keep], axis=1),
    )
    panel_got = lax.ppermute(
        lax.dynamic_slice_in_dim(panel_part, theirs, own_rows, 0), "c", SWAP
    )
    chol_panel = lax.dynamic_slice_in_dim(panel_part, ours, own_rows, 0) + panel_got

    own_index = lax.dynamic_slice_in_dim(row_index, ours, own_rows, 0)
    probe_rest = rademacher(probe_seeds, own_index) - lax.dot_general(
        head_full, chol_panel, (((1,), (1,)), ((), ())), precision=HIGH
    )
    share = block_w // (2 * ranks * 2)
    place = lax.axis_index(("xl", "z", "c")) * share
    head_solve = lax.dynamic_slice_in_dim(head_full, place, share, 1)
    return new_factor, chol_panel, head_solve, probe_rest


def solution(mesh):
    fine = Mesh(mesh.devices.reshape(2, 4, 2, 8, 2), ("xh", "y", "xl", "z", "c"))
    col = ("xl", "z", "c")
    every = ROW + col
    return jax.shard_map(
        local,
        mesh=fine,
        in_specs=(P(col, ROW), P(every, None), P(col, ROW), P()),
        out_specs=(P(every, None), P(every, None), P(None, col), P(None, every)),
        check_vma=False,
    )
```
